32 devices in a mesh: role: 2 (over core), expert: 8 (over z, y), tensor: 2 (over x).
Axes of the slice: x: 2, y: 2, z: 4, core: 2. Of those that a mesh axis runs over, the one named last changes fastest.
Arguments:
- tokens: bfloat16 [512, 2048], P(('role', 'expert'), 'tensor'), may hold values from -180 to 180
- routes: int32 [512, 8], P(('role', 'expert')), may hold values from 0 to 15, all different within a row; in each aligned block of 32 rows (0 to 31, 32 to 63, ...) at most 24 rows name the same one
- gates: float32 [512, 8], P(('role', 'expert')), may hold values from 0.2 to 0.6
- norm_gain: float32 [2048], replicated, may hold values from 0.5 to 2
- w_gate: bfloat16 [16, 768, 2048], P(('role', 'expert'), None, 'tensor'), may hold values from -0.125 to 0.125
- w_up: bfloat16 [16, 768, 2048], P(('role', 'expert'), None, 'tensor'), may hold values from -0.125 to 0.125
- w_down: bfloat16 [16, 768, 2048], P(('role', 'expert'), None, 'tensor'), may hold values from -0.21875 to 0.21875
Outputs:
- moe_out: bfloat16 [512, 2048], P(('role', 'expert'), 'tensor')
The draws below stay inside these ranges and needn't reach their ends.
Inputs may be any that keep to these rules, and one draw needn't show every extreme that they name: `routes`: each row names 8 different experts. Among the rows of one device (aligned blocks of 32 rows) no expert is named by more than 24 rows, and in every draw some block names some expert exactly 24 times.
All inputs are finite; a program needn't handle non-finite values.
Results may differ from the reference program's by a relative error of at most 0.0072.
Values may be sent and summed in bfloat16 or wider, within the bound.
A program may use at most 64 MiB of HBM per device.

```python
import math
import jax
import jax.numpy as jnp
import numpy as np
from jax import lax

D = 2048
EFF = 768
TOP = 8
TOK_DEV = 32
EXPERTS = 16
TOKENS = 512
CAP = 24


def draw_tokens(key, part):
    key = jax.random.fold_in(key, 11)
    key_base, key_cols, key_rows = jax.random.split(key, 3)
    position = jnp.arange(D, dtype=jnp.float32) / D
    col_scale = 10.0 ** (0.5 * position + 0.5 * jax.random.uniform(key_cols, (D,), jnp.float32))
    row_scale = 10.0 ** jax.random.uniform(key_rows, (TOKENS, 1), jnp.float32)
    base = jnp.clip(jax.random.normal(key_base, (TOKENS, D), jnp.float32), -6.0, 6.0)
    return (base * col_scale[None, :] * row_scale * 0.3).astype(jnp.bfloat16)


def block_scale(rng, shape, shards, least, largest):
    factor_of = 1.0
    for dim, blocks in shards:
        draws = jax.random.uniform(jax.random.fold_in(jax.random.fold_in(rng, 6), dim), (blocks,), jnp.float32, least / len(shards), largest / len(shards))
        factor_of = factor_of * jnp.repeat(jnp.exp(draws), shape[dim] // blocks).reshape((-1,) + (1,) * (len(shape) - 1 - dim))
    return factor_of


def routed_block(key, own, number, rows, count, top, bound, slope):
    ranking = jax.random.permutation(key, count)
    packed, ordinary = shares(count, rows * top, bound, slope, True), shares(count, rows * top, bound, slope, False)
    places = jnp.arange(count)

    def named(sizes, rotation):
        used = int((sizes > 0).sum())
        fixed = max(1, used // 4)
        shifted = fixed + (places - fixed + rotation * (used - fixed)) % max(1, count - fixed)
        return jnp.zeros((count,), jnp.int32).at[ranking[jnp.where(places < fixed, places, shifted)]].set(jnp.asarray(sizes, jnp.int32))

    sizes = jnp.where(number % 4 == 0, named(packed, number // 4), named(ordinary, number - number // 4 - 1))
    mixed = jax.random.permutation(jax.random.fold_in(own, 3), count)
    giver, taker = mixed[0:count // 2 * 2:2], mixed[1:count // 2 * 2:2]
    room = jnp.minimum(sizes[giver] - 1, bound - sizes[taker]) // 2
    room = jnp.where((giver == ranking[0]) | (taker == ranking[0]) | (sizes[taker] == 0), 0, jnp.maximum(room, 0))
    shifted = jax.random.randint(jax.random.fold_in(own, 4), (count // 2,), 0, 1 << 20) % (room + 1)
    sizes = sizes.at[giver].add(-shifted).at[taker].add(shifted)
    items = jnp.searchsorted(jnp.cumsum(sizes), jnp.arange(rows * top), side="right").astype(jnp.int32)
    listing = items.reshape(top, rows).T
    listing = listing[jax.random.permutation(jax.random.fold_in(own, 1), rows)]
    rotation = jax.random.randint(jax.random.fold_in(own, 2), (rows, 1), 0, top)
    return jnp.take_along_axis(listing, (jnp.arange(top)[None, :] + rotation) % top, axis=1)


def shares(number_of, total, reach, slope, full):
    loads = [(1 << 20) // math.isqrt(grade ** slope) + 1 for grade in range(1, number_of + 1)]
    largest = reach if full else min(reach, max(-(-total // number_of), total * loads[0] // sum(loads)))
    least = 1 if total - largest >= number_of - 1 else 0
    counts, surplus = [largest] + [least] * (number_of - 1), total - largest - least * (number_of - 1)
    while surplus > 0:
        movable = [i for i in range(1, number_of) if counts[i] < largest] or [i for i in range(1, number_of) if counts[i] < reach]
        pool, left = sum([loads[i] for i in movable]), surplus
        for i in movable:
            extra = min(reach - counts[i], max(1, left * loads[i] // pool), surplus)
            counts[i] = counts[i] + extra
            surplus = surplus - extra
    return np.array(counts)


def gaussian(own_key, shape, scale, limit, cuts=(), held_as=jnp.bfloat16):
    array = scale * jax.random.normal(own_key, shape, jnp.float32)
    if cuts:
        array = array * block_scale(own_key, shape, cuts, -0.22, 0.18)
    return jnp.clip(array, -limit, limit).astype(held_as)


def setup_inputs(seed: int = 0) -> dict:
    key_of = jax.random.split(jax.random.key(seed), 8)
    tokens = draw_tokens(jax.random.fold_in(key_of[7], 71), 0)
    routes_keys = jax.random.split(jax.random.fold_in(key_of[1], 1), TOKENS // TOK_DEV)
    routes_turns = jax.random.permutation(jax.random.fold_in(key_of[1], 3), TOKENS // TOK_DEV)
    routes = jax.vmap(lambda own, number: routed_block(jax.random.fold_in(key_of[1], 2), own, number, TOK_DEV, EXPERTS, TOP, CAP, 2))(routes_keys, routes_turns).reshape((TOKENS, TOP))
    gates = jnp.clip(jnp.exp(math.log(0.6) - 1.0986123 * jax.random.uniform(key_of[2], (TOKENS, TOP), jnp.float32) ** block_scale(key_of[2], (TOKENS, TOP), ((0, 16),), -0.2, 0.2)), 0.2, 0.6)
    norm_gain = jnp.clip(jnp.exp(jax.random.uniform(key_of[3], (D,), jnp.float32, math.log(0.5), math.log(2.0))), 0.5, 2.0)
    w_gate = gaussian(key_of[4], (EXPERTS, EFF, D), D ** -0.5, 0.125, ((0, 16), (2, 2)))
    w_up = gaussian(key_of[5], (EXPERTS, EFF, D), D ** -0.5, 0.125, ((0, 16), (2, 2)))
    w_down = gaussian(key_of[6], (EXPERTS, EFF, D), EFF ** -0.5, 0.21875, ((0, 16), (2, 2)))
    return {"tokens": tokens, "routes": routes, "gates": gates, "norm_gain": norm_gain, "w_gate": w_gate, "w_up": w_up, "w_down": w_down}


def slot_tables(routes, gates):
    devices = TOKENS // TOK_DEV
    picked = routes.reshape(devices, TOK_DEV * TOP).astype(jnp.int32)
    one_hot = (picked[:, :, None] == jnp.arange(EXPERTS, dtype=jnp.int32)[None, None, :]).astype(jnp.int32)
    running = jnp.cumsum(one_hot, axis=1).astype(jnp.int32) - one_hot
    earlier = lax.optimization_barrier(jnp.sum(running * one_hot, axis=2)).astype(jnp.int32)
    slot_ids = (picked * CAP + earlier).astype(jnp.int32)
    owners = jnp.broadcast_to(jnp.arange(devices, dtype=jnp.int32)[:, None], slot_ids.shape)
    token_ids = owners * TOK_DEV + jnp.arange(TOK_DEV * TOP, dtype=jnp.int32)[None, :] // TOP
    table = jnp.full((devices, EXPERTS * CAP), TOKENS, jnp.int32).at[owners, slot_ids].set(token_ids)
    weights = jnp.zeros((devices, EXPERTS * CAP), jnp.float32).at[owners, slot_ids].set(gates.reshape(devices, TOK_DEV * TOP))
    table = table.reshape(devices, EXPERTS, CAP).transpose(1, 0, 2).reshape(EXPERTS, devices * CAP)
    weights = weights.reshape(devices, EXPERTS, CAP).transpose(1, 0, 2).reshape(EXPERTS, devices * CAP)
    return (table, weights)

def reference(tokens, routes, gates, norm_gain, w_gate, w_up, w_down):
    values = tokens.astype(jnp.float32)
    scale = lax.rsqrt(lax.optimization_barrier(jnp.mean(values * values, axis=1, keepdims=True)) + 1e-06)
    normed = (values * scale * norm_gain[None, :]).astype(jnp.bfloat16)
    padded = jnp.concatenate([normed, jnp.zeros((1, D), jnp.bfloat16)], axis=0)
    table, weights = slot_tables(routes, gates)

    def one_expert(total, inputs):
        token_ids, token_weights, gate_w, up_w, down_w = inputs
        rows = padded[token_ids]
        gate = jnp.dot(rows, gate_w.T, preferred_element_type=jnp.float32)
        upward = jnp.dot(rows, up_w.T, preferred_element_type=jnp.float32)
        hidden = (jax.nn.silu(gate) * upward).astype(jnp.bfloat16)
        summed = jnp.dot(hidden, down_w, preferred_element_type=jnp.float32)
        expert_rows = lax.optimization_barrier(summed.astype(jnp.bfloat16)).astype(jnp.float32)
        total = total.at[token_ids].add(token_weights[:, None] * expert_rows, mode='drop')
        return (total, None)
    total, unused = lax.scan(one_expert, jnp.zeros((TOKENS, D), jnp.float32), (table, weights, w_gate, w_up, w_down))
    return total.astype(jnp.bfloat16)
```

```python
import functools

import jax
import jax.numpy as jnp
from jax import lax
from jax.experimental import pallas as pl
from jax.experimental.pallas import tpu as pltpu
from jax.sharding import PartitionSpec as P

MESH = pl.DeviceIdType.MESH
F32 = jnp.float32
BF16 = jnp.bfloat16
LANES = 128


def dot_nt(a, b):
    return lax.dot_general(a, b, (((1,), (1,)), ((), ())), preferred_element_type=F32)


def dot_nn(a, b):
    return jnp.dot(a, b, preferred_element_type=F32)


def moe_kernel(
    n_expert, top_k, capacity,
    tokens, routes, gates, gain, wg_hbm, wu_hbm, wd_hbm, out,
    wg, wu, wd, sq_send, sq_recv, ag, xs, xr, acc, hown, hpeer,
    cs, cr, ck, ys, yr, yk, zs, zr, fin,
    w_sem, send_sem, recv_sem,
):
    role, expert, tensor = lax.axis_index("role"), lax.axis_index("expert"), lax.axis_index("tensor")
    nz = n_expert // 2
    z, y = expert // 2, expert % 2
    width = tokens.shape[1]
    tok = tokens.shape[0]
    experts = 2 * n_expert
    chunk = 4 * tok
    rows = 4 * capacity
    half = wg.shape[0] // 2
    mine = role * n_expert + expert

    mate = (1 - role, expert, tensor)
    across = (role, expert, 1 - tensor)
    ypeer = (role, z * 2 + (1 - y), tensor)

    def zpeer(step):
        return (role, ((z + step) % nz) * 2 + y, tensor)

    weights = [
        pltpu.make_async_copy(src, dst, w_sem.at[i])
        for i, (src, dst) in enumerate(((wg_hbm, wg), (wu_hbm, wu), (wd_hbm, wd)))
    ]
    for copy in weights:
        copy.start()

    barrier = pltpu.get_barrier_semaphore()
    partners = [across, mate, ypeer] + [zpeer(step) for step in range(1, nz)]
    for partner in partners:
        pl.semaphore_signal(barrier, inc=1, device_id=partner, device_id_type=MESH)

    count = [0]
    pending = []

    def remote(src, dst, device):
        i = count[0]
        count[0] += 1
        copy = pltpu.make_async_remote_copy(
            src_ref=src, dst_ref=dst, send_sem=send_sem.at[i], recv_sem=recv_sem.at[i],
            device_id=device, device_id_type=MESH,
        )
        copy.start()
        pending.append(copy)
        return copy

    own = tokens[...].astype(F32)
    part = jnp.sum(own * own, axis=1, keepdims=True)
    sq_send[...] = jnp.broadcast_to(part, (tok, LANES))
    lane = lax.broadcasted_iota(jnp.int32, (tok, LANES), 1)
    dense = jnp.zeros((tok, LANES), F32)
    for k in range(top_k):
        dense = dense + jnp.where(routes[:, k:k + 1] == lane % experts, gates[:, k:k + 1], 0.0)
    high = dense.astype(BF16).astype(F32)
    dense = jnp.where(lane < experts, high, dense - high)
    ag[0, 0, 0, :, width:] = dense.astype(BF16)
    pl.semaphore_wait(barrier, len(partners))
    squares = remote(sq_send, sq_recv, across)
    gained = gain[:, pl.ds(pl.multiple_of(tensor * width, LANES), width)]
    squares.wait_recv()
    total = (part + sq_recv[:, 0:1]) / (2 * width)
    normed = own * lax.rsqrt(total + 1e-06) * gained
    ag[0, 0, 0, :, :width] = normed.astype(BF16)

    in_z, in_y, in_c, in_x, in_h, in_cr, in_yr, in_zr = {}, {}, {}, {}, {}, {}, {}, {}
    picks, scales = {}, {}
    y_first = remote(ag.at[0, 0, 0], ag.at[0, 0, 1], ypeer)
    for s in range(1, nz):
        in_z[s] = remote(ag.at[0, 0, 0], ag.at[s, 0, 0], zpeer(nz - s))
    in_y[0] = y_first
    in_c[0, 0] = remote(ag.at[0, 0, 0], ag.at[0, 1, 0], mate)

    def forward_z(s):
        in_z[s].wait_recv()
        in_y[s] = remote(ag.at[s, 0, 0], ag.at[s, 0, 1], ypeer)
        in_c[s, 0] = remote(ag.at[s, 0, 0], ag.at[s, 1, 0], mate)

    def forward_y(s):
        in_y[s].wait_recv()
        in_c[s, 1] = remote(ag.at[s, 0, 1], ag.at[s, 1, 1], mate)

    row_id = lax.broadcasted_iota(jnp.int32, (chunk, chunk), 0)
    col_id = lax.broadcasted_iota(jnp.int32, (chunk, chunk), 1)
    before = jnp.where(col_id < row_id, 1.0, 0.0).astype(BF16)
    lane_id = lax.broadcasted_iota(jnp.int32, (chunk, LANES), 1)
    own_at = pl.ds(pl.multiple_of(tensor * half, LANES), half)
    peer_at = pl.ds(pl.multiple_of((1 - tensor) * half, LANES), half)

    def project(s):
        in_c[s, 0].wait_recv()
        in_c[s, 1].wait_recv()
        table = ag[s, :, :, :, width:].reshape(chunk, LANES).astype(F32)
        chosen = (lane_id == mine) | (lane_id == experts + mine)
        scale = jnp.sum(jnp.where(chosen, table, 0.0), axis=1, keepdims=True)
        named = jnp.broadcast_to(jnp.where(scale > 0.0, 1.0, 0.0), (chunk, chunk))
        place = dot_nn(before, named.astype(BF16))
        pick = jnp.where(place == col_id.astype(F32), named, 0.0)
        picks[s] = pick.astype(BF16)
        scales[s] = scale
        if s == 0:
            weights[0].wait()
            weights[1].wait()
        block = ag[s, :, :, :, :width].reshape(chunk, width)
        x = dot_nn(pick.T.astype(BF16)[:rows], block).astype(BF16)
        xs[s, :, :half] = dot_nt(x, wg[peer_at, :]).astype(BF16)
        xs[s, :, half:] = dot_nt(x, wu[peer_at, :]).astype(BF16)
        in_x[s] = remote(xs.at[s], xr.at[s], across)
        acc[s, :, :half] = dot_nt(x, wg[own_at, :])
        acc[s, :, half:] = dot_nt(x, wu[own_at, :])

    def activate(s):
        in_x[s].wait_recv()
        gate = acc[s, :, :half] + xr[s, :, :half].astype(F32)
        up = acc[s, :, half:] + xr[s, :, half:].astype(F32)
        hown[s] = (gate / (1.0 + jnp.exp(-gate)) * up).astype(BF16)
        in_h[s] = remote(hown.at[s], hpeer.at[s], across)

    def descend(s):
        if s == 0:
            weights[2].wait()
        result = dot_nn(hown[s], wd[own_at, :])
        in_h[s].wait_recv()
        result = (result + dot_nn(hpeer[s], wd[peer_at, :])).astype(BF16)
        result = jnp.concatenate([result, jnp.zeros((chunk - rows, width), BF16)], axis=0)
        share = dot_nn(picks[s], result) * scales[s]
        cs[s] = share[2 * tok:].astype(BF16)
        in_cr[s] = remote(cs.at[s], cr.at[s], mate)
        ck[s] = share[:2 * tok]

    def return_core(s):
        in_cr[s].wait_recv()
        ys[s] = (ck[s, tok:] + cr[s, tok:].astype(F32)).astype(BF16)
        in_yr[s] = remote(ys.at[s], yr.at[s], ypeer)
        yk[s] = ck[s, :tok] + cr[s, :tok].astype(F32)

    def return_y(s):
        in_yr[s].wait_recv()
        value = yk[s] + yr[s].astype(F32)
        if s == 0:
            fin[...] = value
        else:
            zs[s] = value.astype(BF16)
            in_zr[s] = remote(zs.at[s], zr.at[s], zpeer(s))

    phases = (
        (forward_z, 0), (forward_y, 1), (project, 2), (activate, 4),
        (descend, 6), (return_core, 7), (return_y, 8),
    )
    last = max(delay for _, delay in phases) + nz
    for step in range(last):
        for phase, delay in phases:
            s = step - delay
            if 0 <= s < nz and not (phase is forward_z and s == 0):
                phase(s)

    value = fin[...]
    for s in range(1, nz):
        in_zr[s].wait_recv()
        value = value + zr[s].astype(F32)
    out[...] = value.astype(BF16)
    for copy in pending:
        copy.wait_send()


def gathered(tokens, routes, gates, norm_gain, w_gate, w_up, w_down):
    tok, width = tokens.shape
    top_k = routes.shape[1]
    n_expert = lax.axis_size("expert")
    experts = 2 * n_expert
    capacity = min(tok, max(2, 3 * tok * top_k // (2 * experts)))
    eff = w_gate.shape[1]
    nz, half, rows = n_expert // 2, eff // 2, 4 * capacity
    copies = 1 + (nz - 1) + nz + 2 * nz + 4 * nz + (nz - 1)
    vmem = pl.BlockSpec(memory_space=pltpu.VMEM)
    hbm = pl.BlockSpec(memory_space=pl.ANY)
    return pl.pallas_call(
        functools.partial(moe_kernel, n_expert, top_k, capacity),
        out_shape=jax.ShapeDtypeStruct((tok, width), BF16),
        in_specs=[vmem] * 4 + [hbm] * 3,
        out_specs=vmem,
        scratch_shapes=[
            pltpu.VMEM((eff, width), BF16),
            pltpu.VMEM((eff, width), BF16),
            pltpu.VMEM((eff, width), BF16),
            pltpu.VMEM((tok, LANES), F32),
            pltpu.VMEM((tok, LANES), F32),
            pltpu.VMEM((nz, 2, 2, tok, width + LANES), BF16),
            pltpu.VMEM((nz, rows, eff), BF16),
            pltpu.VMEM((nz, rows, eff), BF16),
            pltpu.VMEM((nz, rows, eff), F32),
            pltpu.VMEM((nz, rows, half), BF16),
            pltpu.VMEM((nz, rows, half), BF16),
            pltpu.VMEM((nz, 2 * tok, width), BF16),
            pltpu.VMEM((nz, 2 * tok, width), BF16),
            pltpu.VMEM((nz, 2 * tok, width), F32),
            pltpu.VMEM((nz, tok, width), BF16),
            pltpu.VMEM((nz, tok, width), BF16),
            pltpu.VMEM((nz, tok, width), F32),
            pltpu.VMEM((nz, tok, width), BF16),
            pltpu.VMEM((nz, tok, width), BF16),
            pltpu.VMEM((tok, width), F32),
            pltpu.SemaphoreType.DMA((3,)),
            pltpu.SemaphoreType.DMA((copies,)),
            pltpu.SemaphoreType.DMA((copies,)),
        ],
        compiler_params=pltpu.CompilerParams(
            collective_id=0, has_side_effects=True, vmem_limit_bytes=40 * 1024 * 1024
        ),
    )(
        tokens, routes, gates, norm_gain.reshape(1, -1),
        w_gate.reshape(eff, width), w_up.reshape(eff, width), w_down.reshape(eff, width),
    )


def takes_gathered(mesh, tokens, routes, w_gate):
    sizes = mesh.shape
    groups = sizes["role"] * sizes["expert"]
    tok, top_k, experts = tokens.shape[0] // groups, routes.shape[1], w_gate.shape[0]
    capacity = min(tok, max(2, 3 * tok * top_k // (2 * experts)))
    return (
        sizes["role"] == 2 and sizes["tensor"] == 2 and sizes["expert"] % 2 == 0
        and experts == groups and 2 * top_k >= experts and 2 * experts <= LANES
        and 4 * tok == LANES and capacity % 4 == 0 and w_gate.shape[1] % (2 * LANES) == 0
        and tokens.shape[1] % (2 * LANES) == 0
    )


def expert_ffn(arrived, w_gate, w_up, w_down):
    gate = jnp.einsum("sekq,efq->sekf", arrived, w_gate, preferred_element_type=jnp.float32)
    upward = jnp.einsum("sekq,efq->sekf", arrived, w_up, preferred_element_type=jnp.float32)
    gate, upward = lax.psum((gate, upward), "tensor")
    hidden = (jax.nn.silu(gate) * upward).astype(jnp.bfloat16)
    output = jnp.einsum("sekf,efq->sekq", hidden, w_down, preferred_element_type=jnp.float32)
    return output.astype(jnp.bfloat16)


def per_device(tokens, routes, gates, norm_gain, w_gate, w_up, w_down):
    tok_dev, quarter = tokens.shape
    top_k = routes.shape[1]
    exp_dev = w_gate.shape[0]
    n_role = lax.axis_size("role")
    n_expert = lax.axis_size("expert")
    n_tensor = lax.axis_size("tensor")
    devices = n_role * n_expert
    experts = exp_dev * devices
    capacity = min(tok_dev, max(2, 3 * tok_dev * top_k // (2 * experts)))
    width = quarter * n_tensor
    slots = experts * capacity
    picked = routes.reshape(-1)
    one_hot = (picked[:, None] == jnp.arange(experts, dtype=jnp.int32)[None, :]).astype(jnp.int32)
    running = jnp.cumsum(one_hot, axis=0) - one_hot
    earlier = jnp.sum(running * one_hot, axis=1)
    slot_ids = (picked * capacity + earlier).reshape(tok_dev, top_k)
    matches = slot_ids[:, None, :] == jnp.arange(slots, dtype=jnp.int32)[None, :, None]
    pick_rows = jnp.sum(matches.astype(jnp.float32), axis=2).astype(jnp.bfloat16)
    combine = jnp.sum(jnp.where(matches, gates[:, None, :], 0.0), axis=2)
    own = tokens.astype(jnp.float32)
    squares = lax.psum(jnp.sum(own * own, axis=1), "tensor")
    scale = lax.rsqrt(squares / width + 1e-06)[:, None]
    gain_part = lax.dynamic_slice_in_dim(norm_gain, lax.axis_index("tensor") * quarter, quarter)
    normed = (own * scale * gain_part[None, :]).astype(jnp.bfloat16)
    outgoing = jnp.einsum(
        "ts,td->sd", pick_rows, normed, preferred_element_type=jnp.float32
    ).astype(jnp.bfloat16)
    outgoing = outgoing.reshape(devices, exp_dev, capacity, quarter)
    results = expert_ffn(
        lax.all_to_all(outgoing, ("role", "expert"), split_axis=0, concat_axis=0, tiled=True),
        w_gate,
        w_up,
        w_down,
    )
    returned = lax.all_to_all(results, ("role", "expert"), split_axis=0, concat_axis=0, tiled=True)
    returned = returned.reshape(slots, quarter).astype(jnp.float32)
    mixed = jnp.dot(
        combine, returned, precision=lax.Precision.HIGHEST, preferred_element_type=jnp.float32
    )
    return mixed.astype(jnp.bfloat16)


def solution(mesh):
    in_specs = (
        P(("role", "expert"), "tensor"),
        P(("role", "expert"), None),
        P(("role", "expert"), None),
        P(),
        P(("role", "expert"), None, "tensor"),
        P(("role", "expert"), None, "tensor"),
        P(("role", "expert"), None, "tensor"),
    )
    out_specs = P(("role", "expert"), "tensor")

    def layer(tokens, routes, gates, norm_gain, w_gate, w_up, w_down):
        body = gathered if takes_gathered(mesh, tokens, routes, w_gate) else per_device
        return jax.shard_map(
            body, mesh=mesh, in_specs=in_specs, out_specs=out_specs, check_vma=False
        )(tokens, routes, gates, norm_gain, w_gate, w_up, w_down)

    return layer
```

```python
import functools

import jax
import jax.numpy as jnp
from jax import lax
from jax.experimental import pallas as pl
from jax.experimental.pallas import tpu as pltpu
from jax.sharding import PartitionSpec as P

MESH = pl.DeviceIdType.MESH
F32 = jnp.float32
BF16 = jnp.bfloat16
LANES = 128
LAG = (1, 2, 3, 4)


def dot_nt(a, b):
    return lax.dot_general(a, b, (((1,), (1,)), ((), ())), preferred_element_type=F32)


def dot_nn(a, b):
    return jnp.dot(a, b, preferred_element_type=F32)


def moe_kernel(
    n_expert, top_k, capacity,
    tokens_hbm, routes_hbm, gates_hbm, gain_hbm, wg_hbm, wu_hbm, wd_hbm, out,
    tokens, routes, gates, gain, wg, wu, wd, sq_send, sq_recv, ag, xs, xr, acc, hown, hpeer,
    cs, cr, ck, ys, yr, yk, zs, zr,
    w_sem, send_sem, recv_sem,
):
    role, expert, tensor = lax.axis_index("role"), lax.axis_index("expert"), lax.axis_index("tensor")
    nz = n_expert // 2
    z, y = expert // 2, expert % 2
    tok, width = tokens.shape
    experts = 2 * n_expert
    half = wg.shape[0] // 2
    mine = role * n_expert + expert

    mate = (1 - role, expert, tensor)
    across = (role, expert, 1 - tensor)
    ypeer = (role, z * 2 + (1 - y), tensor)

    def zpeer(step):
        return (role, ((z + step) % nz) * 2 + y, tensor)

    barrier = pltpu.get_barrier_semaphore()
    partners = [across, mate, ypeer] + [zpeer(step) for step in range(1, nz)]
    for partner in partners:
        pl.semaphore_signal(barrier, inc=1, device_id=partner, device_id_type=MESH)

    gain_part = gain_hbm.at[:, pl.ds(pl.multiple_of(tensor * width, LANES), width)]
    loads = [
        pltpu.make_async_copy(src, dst, w_sem.at[i])
        for i, (src, dst) in enumerate((
            (tokens_hbm, tokens), (routes_hbm, routes), (gates_hbm, gates), (gain_part, gain),
            (wg_hbm, wg), (wu_hbm, wu), (wd_hbm, wd),
        ))
    ]
    for copy in loads:
        copy.start()

    count = [0]
    pending = []

    def remote(src, dst, device):
        i = count[0]
        count[0] += 1
        copy = pltpu.make_async_remote_copy(
            src_ref=src, dst_ref=dst, send_sem=send_sem.at[i], recv_sem=recv_sem.at[i],
            device_id=device, device_id_type=MESH,
        )
        copy.start()
        pending.append(copy)
        return copy

    loads[0].wait()
    own = tokens[...].astype(F32)
    part = jnp.sum(own * own, axis=1, keepdims=True)
    sq_send[...] = jnp.broadcast_to(part, (tok, LANES))
    pl.semaphore_wait(barrier, len(partners))
    squares = remote(sq_send, sq_recv, across)

    loads[1].wait()
    loads[2].wait()
    loads[3].wait()
    entry = lax.broadcasted_iota(jnp.int32, (LANES, tok), 0)
    dense = jnp.zeros((LANES, tok), F32)
    for k in range(top_k):
        dense = dense + jnp.where(routes[k:k + 1, :] == entry % experts, gates[k:k + 1, :], 0.0)
    high = dense.astype(BF16).astype(F32)
    dense = jnp.where(entry < experts, high, dense - high)
    ag[0, 0, 0, :, width:] = dense.T.astype(BF16)
    gained = gain[...]
    squares.wait_recv()
    total = (part + sq_recv[:, 0:1]) / (2 * width)
    normed = own * lax.rsqrt(total + 1e-06) * gained
    ag[0, 0, 0, :, :width] = normed.astype(BF16)

    in_z, in_y, in_c, in_x, in_h, in_cr, in_yr, in_zr = {}, {}, {}, {}, {}, {}, {}, {}
    picks, scales = {}, {}
    in_y[0] = remote(ag.at[0, 0, 0], ag.at[0, 1, 0], ypeer)
    near = sorted(range(1, nz), key=lambda s: min(s, nz - s))
    waves = [[s for s in near if min(s, nz - s) == d] for d in range(1, nz // 2 + 1)]

    def send_wave(number):
        if number:
            for s in waves[number - 1]:
                in_z[s].wait_send()
                pending[:] = [copy for copy in pending if copy is not in_z[s]]
        for s in waves[number]:
            in_z[s] = remote(ag.at[0, 0, 0], ag.at[s, 0, 0], zpeer(nz - s))

    if waves:
        send_wave(0)
    in_c[0, 0] = remote(ag.at[0, 0, 0], ag.at[0, 0, 1], mate)

    def forward_z(s):
        in_z[s].wait_recv()
        in_y[s] = remote(ag.at[s, 0, 0], ag.at[s, 1, 0], ypeer)
        in_c[s, 0] = remote(ag.at[s, 0, 0], ag.at[s, 0, 1], mate)

    def forward_y(s):
        in_y[s].wait_recv()
        in_c[s, 1] = remote(ag.at[s, 1, 0], ag.at[s, 1, 1], mate)

    own_at = pl.ds(pl.multiple_of(tensor * half, LANES), half)
    peer_at = pl.ds(pl.multiple_of((1 - tensor) * half, LANES), half)
    groups = [(0, 0, 1), (0, 1, 1)] + [(s, 0, 2) for s in near]

    def project(g):
        s, first, many = groups[g]
        at = pl.ds(first, many)
        for i in range(first, first + many):
            in_c[s, i].wait_recv()
        chunk, rows = many * 2 * tok, many * 2 * capacity
        table = ag[s, at, :, :, width:].reshape(chunk, LANES).astype(F32)
        lane = lax.broadcasted_iota(jnp.int32, (chunk, LANES), 1)
        chosen = (lane == mine) | (lane == experts + mine)
        scale = jnp.sum(jnp.where(chosen, table, 0.0), axis=1, keepdims=True)
        named = jnp.broadcast_to(jnp.where(scale > 0.0, 1.0, 0.0), (chunk, LANES))
        row_id = lax.broadcasted_iota(jnp.int32, (chunk, chunk), 0)
        col_id = lax.broadcasted_iota(jnp.int32, (chunk, chunk), 1)
        before = jnp.where(col_id < row_id, 1.0, 0.0).astype(BF16)
        place = dot_nn(before, named.astype(BF16))
        pick = jnp.where(place == lane.astype(F32), named, 0.0)
        picks[g] = pick.astype(BF16)
        scales[g] = scale
        if g == 0:
            loads[4].wait()
            loads[5].wait()
        block = ag[s, at, :, :, :width].reshape(chunk, width)
        x = dot_nn(pick.T.astype(BF16)[:rows], block).astype(BF16)
        shape = (many, 2 * capacity, half)
        xs[s, at, :, :half] = dot_nt(x, wg[peer_at, :]).astype(BF16).reshape(shape)
        xs[s, at, :, half:] = dot_nt(x, wu[peer_at, :]).astype(BF16).reshape(shape)
        in_x[g] = remote(xs.at[s, at], xr.at[s, at], across)
        acc[s, at, :, :half] = dot_nt(x, wg[own_at, :]).reshape(shape)
        acc[s, at, :, half:] = dot_nt(x, wu[own_at, :]).reshape(shape)

    def activate(g):
        s, first, many = groups[g]
        at = pl.ds(first, many)
        in_x[g].wait_recv()
        gate = acc[s, at, :, :half] + xr[s, at, :, :half].astype(F32)
        up = acc[s, at, :, half:] + xr[s, at, :, half:].astype(F32)
        hown[s, at] = (gate / (1.0 + jnp.exp(-gate)) * up).astype(BF16)
        in_h[g] = remote(hown.at[s, at], hpeer.at[s, at], across)

    def descend(g):
        s, first, many = groups[g]
        at = pl.ds(first, many)
        rows = many * 2 * capacity
        if g == 0:
            loads[6].wait()
        result = dot_nn(hown[s, at].reshape(rows, half), wd[own_at, :])
        in_h[g].wait_recv()
        result = (result + dot_nn(hpeer[s, at].reshape(rows, half), wd[peer_at, :])).astype(BF16)
        result = jnp.concatenate([result, jnp.zeros((LANES - rows, width), BF16)], axis=0)
        share = (dot_nn(picks[g], result) * scales[g]).reshape(many, 2, tok, width)
        cs[s, at] = share[:, 1].astype(BF16)
        in_cr[g] = remote(cs.at[s, at], cr.at[s, at], mate)
        ck[s, at] = share[:, 0]

    def return_core(g):
        s, first, many = groups[g]
        in_cr[g].wait_recv()
        for i in reversed(range(first, first + many)):
            value = ck[s, i] + cr[s, i].astype(F32)
            if i == 1:
                ys[s] = value.astype(BF16)
                in_yr[s] = remote(ys.at[s], yr.at[s], ypeer)
            else:
                yk[s] = value

    def return_y(s):
        in_yr[s].wait_recv()
        zs[s] = (yk[s] + yr[s].astype(F32)).astype(BF16)
        in_zr[s] = remote(zs.at[s], zr.at[s], zpeer(s))

    n = len(groups)

    def ready_z(g):
        if g < n and groups[g][0] and groups[g][1] == 0:
            forward_z(groups[g][0])

    def ready_y(g):
        if g < n and sum(groups[g][1:]) == 2:
            forward_y(groups[g][0])

    def finish(g):
        if groups[g][0]:
            return_y(groups[g][0])

    ready_z(0)
    ready_y(0)
    for step in range(n + LAG[3]):
        if step < n:
            project(step)
            if step + 1 < len(waves):
                send_wave(step + 1)
            if step == 0:
                ready_z(1)
            ready_z(step + 2)
            ready_y(step + 1)
        for phase, delay in zip((activate, descend, return_core, finish), LAG):
            if 0 <= step - delay < n:
                phase(step - delay)

    value = yk[0]
    in_yr[0].wait_recv()
    value = value + yr[0].astype(F32)
    for s in range(1, nz):
        in_zr[s].wait_recv()
        value = value + zr[s].astype(F32)
    out[...] = value.astype(BF16)
    for copy in pending:
        copy.wait_send()


def gathered(tokens, routes, gates, norm_gain, w_gate, w_up, w_down):
    tok, width = tokens.shape
    top_k = routes.shape[1]
    n_expert = lax.axis_size("expert")
    experts = 2 * n_expert
    capacity = min(tok, max(2, 3 * tok * top_k // (2 * experts)))
    eff = w_gate.shape[1]
    nz, half, rows = n_expert // 2, eff // 2, 2 * capacity
    copies = 1 + (nz - 1) + nz + 2 * nz + 3 * (nz + 1) + nz + (nz - 1)
    vmem = pl.BlockSpec(memory_space=pltpu.VMEM)
    hbm = pl.BlockSpec(memory_space=pl.ANY)
    return pl.pallas_call(
        functools.partial(moe_kernel, n_expert, top_k, capacity),
        out_shape=jax.ShapeDtypeStruct((tok, width), BF16),
        in_specs=[hbm] * 7,
        out_specs=vmem,
        scratch_shapes=[
            pltpu.VMEM((tok, width), BF16),
            pltpu.VMEM((top_k, tok), jnp.int32),
            pltpu.VMEM((top_k, tok), F32),
            pltpu.VMEM((1, width), F32),
            pltpu.VMEM((eff, width), BF16),
            pltpu.VMEM((eff, width), BF16),
            pltpu.VMEM((eff, width), BF16),
            pltpu.VMEM((tok, LANES), F32),
            pltpu.VMEM((tok, LANES), F32),
            pltpu.VMEM((nz, 2, 2, tok, width + LANES), BF16),
            pltpu.VMEM((nz, 2, rows, eff), BF16),
            pltpu.VMEM((nz, 2, rows, eff), BF16),
            pltpu.VMEM((nz, 2, rows, eff), F32),
            pltpu.VMEM((nz, 2, rows, half), BF16),
            pltpu.VMEM((nz, 2, rows, half), BF16),
            pltpu.VMEM((nz, 2, tok, width), BF16),
            pltpu.VMEM((nz, 2, tok, width), BF16),
            pltpu.VMEM((nz, 2, tok, width), F32),
            pltpu.VMEM((nz, tok, width), BF16),
            pltpu.VMEM((nz, tok, width), BF16),
            pltpu.VMEM((nz, tok, width), F32),
            pltpu.VMEM((nz, tok, width), BF16),
            pltpu.VMEM((nz, tok, width), BF16),
            pltpu.SemaphoreType.DMA((7,)),
            pltpu.SemaphoreType.DMA((copies,)),
            pltpu.SemaphoreType.DMA((copies,)),
        ],
        compiler_params=pltpu.CompilerParams(
            collective_id=0, has_side_effects=True, vmem_limit_bytes=63 * 1024 * 1024
        ),
    )(
        tokens, routes.T, gates.T, norm_gain.reshape(1, -1),
        w_gate.reshape(eff, width), w_up.reshape(eff, width), w_down.reshape(eff, width),
    )


def takes_gathered(mesh, tokens, routes, w_gate):
    sizes = mesh.shape
    groups = sizes["role"] * sizes["expert"]
    tok, top_k, experts = tokens.shape[0] // groups, routes.shape[1], w_gate.shape[0]
    capacity = min(tok, max(2, 3 * tok * top_k // (2 * experts)))
    return (
        sizes["role"] == 2 and sizes["tensor"] == 2 and sizes["expert"] % 2 == 0
        and experts == groups and 2 * top_k >= experts and 2 * experts <= LANES
        and 4 * tok == LANES and capacity % 4 == 0 and w_gate.shape[1] % (2 * LANES) == 0
        and tokens.shape[1] % (2 * LANES) == 0
    )


def expert_ffn(arrived, w_gate, w_up, w_down):
    gate = jnp.einsum("sekq,efq->sekf", arrived, w_gate, preferred_element_type=jnp.float32)
    upward = jnp.einsum("sekq,efq->sekf", arrived, w_up, preferred_element_type=jnp.float32)
    gate, upward = lax.psum((gate, upward), "tensor")
    hidden = (jax.nn.silu(gate) * upward).astype(jnp.bfloat16)
    output = jnp.einsum("sekf,efq->sekq", hidden, w_down, preferred_element_type=jnp.float32)
    return output.astype(jnp.bfloat16)


def per_device(tokens, routes, gates, norm_gain, w_gate, w_up, w_down):
    tok_dev, quarter = tokens.shape
    top_k = routes.shape[1]
    exp_dev = w_gate.shape[0]
    n_role = lax.axis_size("role")
    n_expert = lax.axis_size("expert")
    n_tensor = lax.axis_size("tensor")
    devices = n_role * n_expert
    experts = exp_dev * devices
    capacity = min(tok_dev, max(2, 3 * tok_dev * top_k // (2 * experts)))
    width = quarter * n_tensor
    slots = experts * capacity
    picked = routes.reshape(-1)
    one_hot = (picked[:, None] == jnp.arange(experts, dtype=jnp.int32)[None, :]).astype(jnp.int32)
    running = jnp.cumsum(one_hot, axis=0) - one_hot
    earlier = jnp.sum(running * one_hot, axis=1)
    slot_ids = (picked * capacity + earlier).reshape(tok_dev, top_k)
    matches = slot_ids[:, None, :] == jnp.arange(slots, dtype=jnp.int32)[None, :, None]
    pick_rows = jnp.sum(matches.astype(jnp.float32), axis=2).astype(jnp.bfloat16)
    combine = jnp.sum(jnp.where(matches, gates[:, None, :], 0.0), axis=2)
    own = tokens.astype(jnp.float32)
    squares = lax.psum(jnp.sum(own * own, axis=1), "tensor")
    scale = lax.rsqrt(squares / width + 1e-06)[:, None]
    gain_part = lax.dynamic_slice_in_dim(norm_gain, lax.axis_index("tensor") * quarter, quarter)
    normed = (own * scale * gain_part[None, :]).astype(jnp.bfloat16)
    outgoing = jnp.einsum(
        "ts,td->sd", pick_rows, normed, preferred_element_type=jnp.float32
    ).astype(jnp.bfloat16)
    outgoing = outgoing.reshape(devices, exp_dev, capacity, quarter)
    results = expert_ffn(
        lax.all_to_all(outgoing, ("role", "expert"), split_axis=0, concat_axis=0, tiled=True),
        w_gate,
        w_up,
        w_down,
    )
    returned = lax.all_to_all(results, ("role", "expert"), split_axis=0, concat_axis=0, tiled=True)
    returned = returned.reshape(slots, quarter).astype(jnp.float32)
    mixed = jnp.dot(
        combine, returned, precision=lax.Precision.HIGHEST, preferred_element_type=jnp.float32
    )
    return mixed.astype(jnp.bfloat16)


def solution(mesh):
    in_specs = (
        P(("role", "expert"), "tensor"),
        P(("role", "expert"), None),
        P(("role", "expert"), None),
        P(),
        P(("role", "expert"), None, "tensor"),
        P(("role", "expert"), None, "tensor"),
        P(("role", "expert"), None, "tensor"),
    )
    out_specs = P(("role", "expert"), "tensor")

    def layer(tokens, routes, gates, norm_gain, w_gate, w_up, w_down):
        body = gathered if takes_gathered(mesh, tokens, routes, w_gate) else per_device
        return jax.shard_map(
            body, mesh=mesh, in_specs=in_specs, out_specs=out_specs, check_vma=False
        )(tokens, routes, gates, norm_gain, w_gate, w_up, w_down)

    return layer
```

```python
import functools

import jax
import jax.numpy as jnp
from jax import lax
from jax.experimental import pallas as pl
from jax.experimental.pallas import tpu as pltpu
from jax.sharding import PartitionSpec as P

MESH = pl.DeviceIdType.MESH
F32 = jnp.float32
BF16 = jnp.bfloat16
LANES = 128
LAG = (1, 2, 3, 4)


def dot_nt(a, b):
    return lax.dot_general(a, b, (((1,), (1,)), ((), ())), preferred_element_type=F32)


def dot_nn(a, b):
    return jnp.dot(a, b, preferred_element_type=F32)


def moe_kernel(
    n_expert, top_k, capacity,
    tokens_hbm, routes_hbm, gates_hbm, gain_hbm, wg_hbm, wu_hbm, wd_hbm, out,
    tokens, routes, gates, gain, wg, wu, wd, sq_send, sq_recv, ag, xs, xr, acc, hown, hpeer,
    cs, cr, ck, ys, yr, yk, zs, zr,
    w_sem, send_sem, recv_sem,
):
    role, expert, tensor = lax.axis_index("role"), lax.axis_index("expert"), lax.axis_index("tensor")
    nz = n_expert // 2
    z, y = expert // 2, expert % 2
    tok, width = tokens.shape
    experts = 2 * n_expert
    half = wg.shape[0] // 2
    mine = role * n_expert + expert

    mate = (1 - role, expert, tensor)
    across = (role, expert, 1 - tensor)
    ypeer = (role, z * 2 + (1 - y), tensor)

    def zpeer(step):
        return (role, ((z + step) % nz) * 2 + y, tensor)

    barrier = pltpu.get_barrier_semaphore()
    partners = [across, mate, ypeer] + [zpeer(step) for step in range(1, nz)]
    for partner in partners:
        pl.semaphore_signal(barrier, inc=1, device_id=partner, device_id_type=MESH)

    gain_part = gain_hbm.at[:, pl.ds(pl.multiple_of(tensor * width, LANES), width)]
    loads = [
        pltpu.make_async_copy(src, dst, w_sem.at[i])
        for i, (src, dst) in enumerate((
            (tokens_hbm, tokens), (routes_hbm, routes), (gates_hbm, gates), (gain_part, gain),
            (wg_hbm, wg), (wu_hbm, wu), (wd_hbm, wd),
        ))
    ]
    for copy in loads:
        copy.start()

    count = [0]
    pending = []

    def remote(src, dst, device):
        i = count[0]
        count[0] += 1
        copy = pltpu.make_async_remote_copy(
            src_ref=src, dst_ref=dst, send_sem=send_sem.at[i], recv_sem=recv_sem.at[i],
            device_id=device, device_id_type=MESH,
        )
        copy.start()
        pending.append(copy)
        return copy

    loads[0].wait()
    own = tokens[...].astype(F32)
    part = jnp.sum(own * own, axis=1, keepdims=True)
    sq_send[...] = jnp.broadcast_to(part, (tok, LANES))
    pl.semaphore_wait(barrier, len(partners))
    squares = remote(sq_send, sq_recv, across)

    loads[1].wait()
    loads[2].wait()
    loads[3].wait()
    entry = lax.broadcasted_iota(jnp.int32, (LANES, tok), 0)
    dense = jnp.zeros((LANES, tok), F32)
    for k in range(top_k):
        dense = dense + jnp.where(routes[k:k + 1, :] == entry % experts, gates[k:k + 1, :], 0.0)
    high = dense.astype(BF16).astype(F32)
    dense = jnp.where(entry < experts, high, dense - high)
    ag[0, 0, 0, :, width:] = dense.T.astype(BF16)
    gained = gain[...]
    squares.wait_recv()
    total = (part + sq_recv[:, 0:1]) / (2 * width)
    normed = own * lax.rsqrt(total + 1e-06) * gained
    ag[0, 0, 0, :, :width] = normed.astype(BF16)

    in_z, in_y, in_c, in_x, in_h, in_cr, in_yr, in_zr = {}, {}, {}, {}, {}, {}, {}, {}
    picks, scales = {}, {}
    in_c[0, 0] = remote(ag.at[0, 0, 0], ag.at[0, 0, 1], mate)
    in_y[0] = remote(ag.at[0, 0, 0], ag.at[0, 1, 0], ypeer)
    near = sorted(range(1, nz), key=lambda s: min(s, nz - s))
    waves = [[s for s in near if min(s, nz - s) == d] for d in range(1, nz // 2 + 1)]

    def send_wave(number):
        if number:
            for s in waves[number - 1]:
                in_z[s].wait_send()
                pending[:] = [copy for copy in pending if copy is not in_z[s]]
        for s in waves[number]:
            in_z[s] = remote(ag.at[0, 0, 0], ag.at[s, 0, 0], zpeer(nz - s))

    if waves:
        send_wave(0)

    def forward_z(s):
        in_z[s].wait_recv()
        in_y[s] = remote(ag.at[s, 0, 0], ag.at[s, 1, 0], ypeer)
        in_c[s, 0] = remote(ag.at[s, 0, 0], ag.at[s, 0, 1], mate)

    def forward_y(s):
        in_y[s].wait_recv()
        in_c[s, 1] = remote(ag.at[s, 1, 0], ag.at[s, 1, 1], mate)

    own_at = pl.ds(pl.multiple_of(tensor * half, LANES), half)
    peer_at = pl.ds(pl.multiple_of((1 - tensor) * half, LANES), half)
    groups = [(0, 0, 1), (0, 1, 1)] + [(s, 0, 2) for s in near]

    def project(g):
        s, first, many = groups[g]
        at = pl.ds(first, many)
        for i in range(first, first + many):
            in_c[s, i].wait_recv()
        chunk, rows = many * 2 * tok, many * 2 * capacity
        table = ag[s, at, :, :, width:].reshape(chunk, LANES).astype(F32)
        lane = lax.broadcasted_iota(jnp.int32, (chunk, LANES), 1)
        chosen = (lane == mine) | (lane == experts + mine)
        scale = jnp.sum(jnp.where(chosen, table, 0.0), axis=1, keepdims=True)
        named = jnp.broadcast_to(jnp.where(scale > 0.0, 1.0, 0.0), (chunk, LANES))
        row_id = lax.broadcasted_iota(jnp.int32, (chunk, chunk), 0)
        col_id = lax.broadcasted_iota(jnp.int32, (chunk, chunk), 1)
        before = jnp.where(col_id < row_id, 1.0, 0.0).astype(BF16)
        place = dot_nn(before, named.astype(BF16))
        pick = jnp.where(place == lane.astype(F32), named, 0.0)
        picks[g] = pick.astype(BF16)
        scales[g] = scale
        if g == 0:
            loads[4].wait()
            loads[5].wait()
        block = ag[s, at, :, :, :width].reshape(chunk, width)
        x = dot_nn(pick.T.astype(BF16)[:rows], block).astype(BF16)
        shape = (many, 2 * capacity, half)
        xs[s, at, :, :half] = dot_nt(x, wg[peer_at, :]).astype(BF16).reshape(shape)
        xs[s, at, :, half:] = dot_nt(x, wu[peer_at, :]).astype(BF16).reshape(shape)
        in_x[g] = remote(xs.at[s, at], xr.at[s, at], across)
        acc[s, at, :, :half] = dot_nt(x, wg[own_at, :]).reshape(shape)
        acc[s, at, :, half:] = dot_nt(x, wu[own_at, :]).reshape(shape)

    def activate(g):
        s, first, many = groups[g]
        at = pl.ds(first, many)
        in_x[g].wait_recv()
        gate = acc[s, at, :, :half] + xr[s, at, :, :half].astype(F32)
        up = acc[s, at, :, half:] + xr[s, at, :, half:].astype(F32)
        hown[s, at] = (gate / (1.0 + jnp.exp(-gate)) * up).astype(BF16)
        in_h[g] = remote(hown.at[s, at], hpeer.at[s, at], across)

    def descend(g):
        s, first, many = groups[g]
        at = pl.ds(first, many)
        rows = many * 2 * capacity
        if g == 0:
            loads[6].wait()
        result = dot_nn(hown[s, at].reshape(rows, half), wd[own_at, :])
        in_h[g].wait_recv()
        result = (result + dot_nn(hpeer[s, at].reshape(rows, half), wd[peer_at, :])).astype(BF16)
        result = jnp.concatenate([result, jnp.zeros((LANES - rows, width), BF16)], axis=0)
        share = (dot_nn(picks[g], result) * scales[g]).reshape(many, 2, tok, width)
        cs[s, at] = share[:, 1].astype(BF16)
        in_cr[g] = remote(cs.at[s, at], cr.at[s, at], mate)
        ck[s, at] = share[:, 0]

    def return_core(g):
        s, first, many = groups[g]
        in_cr[g].wait_recv()
        for i in reversed(range(first, first + many)):
            value = ck[s, i] + cr[s, i].astype(F32)
            if i == 1:
                ys[s] = value.astype(BF16)
                in_yr[s] = remote(ys.at[s], yr.at[s], ypeer)
            else:
                yk[s] = value

    def return_y(s):
        in_yr[s].wait_recv()
        zs[s] = (yk[s] + yr[s].astype(F32)).astype(BF16)
        in_zr[s] = remote(zs.at[s], zr.at[s], zpeer(s))

    n = len(groups)

    def ready_z(g):
        if g < n and groups[g][0] and groups[g][1] == 0:
            forward_z(groups[g][0])

    def ready_y(g):
        if g < n and sum(groups[g][1:]) == 2:
            forward_y(groups[g][0])

    def finish(g):
        if groups[g][0]:
            return_y(groups[g][0])

    ready_z(0)
    ready_y(0)
    for step in range(n + LAG[3]):
        if step < n:
            project(step)
            if step + 1 < len(waves):
                send_wave(step + 1)
            if step == 0:
                ready_z(1)
            ready_z(step + 2)
            ready_y(step + 1)
        for phase, delay in zip((activate, descend, return_core, finish), LAG):
            if 0 <= step - delay < n:
                phase(step - delay)

    value = yk[0]
    in_yr[0].wait_recv()
    value = value + yr[0].astype(F32)
    for s in range(1, nz):
        in_zr[s].wait_recv()
        value = value + zr[s].astype(F32)
    out[...] = value.astype(BF16)
    for copy in pending:
        copy.wait_send()


def gathered(tokens, routes, gates, norm_gain, w_gate, w_up, w_down):
    tok, width = tokens.shape
    top_k = routes.shape[1]
    n_expert = lax.axis_size("expert")
    experts = 2 * n_expert
    capacity = min(tok, max(2, 3 * tok * top_k // (2 * experts)))
    eff = w_gate.shape[1]
    nz, half, rows = n_expert // 2, eff // 2, 2 * capacity
    copies = 1 + (nz - 1) + nz + 2 * nz + 3 * (nz + 1) + nz + (nz - 1)
    vmem = pl.BlockSpec(memory_space=pltpu.VMEM)
    hbm = pl.BlockSpec(memory_space=pl.ANY)
    return pl.pallas_call(
        functools.partial(moe_kernel, n_expert, top_k, capacity),
        out_shape=jax.ShapeDtypeStruct((tok, width), BF16),
        in_specs=[hbm] * 7,
        out_specs=vmem,
        scratch_shapes=[
            pltpu.VMEM((tok, width), BF16),
            pltpu.VMEM((top_k, tok), jnp.int32),
            pltpu.VMEM((top_k, tok), F32),
            pltpu.VMEM((1, width), F32),
            pltpu.VMEM((eff, width), BF16),
            pltpu.VMEM((eff, width), BF16),
            pltpu.VMEM((eff, width), BF16),
            pltpu.VMEM((tok, LANES), F32),
            pltpu.VMEM((tok, LANES), F32),
            pltpu.VMEM((nz, 2, 2, tok, width + LANES), BF16),
            pltpu.VMEM((nz, 2, rows, eff), BF16),
            pltpu.VMEM((nz, 2, rows, eff), BF16),
            pltpu.VMEM((nz, 2, rows, eff), F32),
            pltpu.VMEM((nz, 2, rows, half), BF16),
            pltpu.VMEM((nz, 2, rows, half), BF16),
            pltpu.VMEM((nz, 2, tok, width), BF16),
            pltpu.VMEM((nz, 2, tok, width), BF16),
            pltpu.VMEM((nz, 2, tok, width), F32),
            pltpu.VMEM((nz, tok, width), BF16),
            pltpu.VMEM((nz, tok, width), BF16),
            pltpu.VMEM((nz, tok, width), F32),
            pltpu.VMEM((nz, tok, width), BF16),
            pltpu.VMEM((nz, tok, width), BF16),
            pltpu.SemaphoreType.DMA((7,)),
            pltpu.SemaphoreType.DMA((copies,)),
            pltpu.SemaphoreType.DMA((copies,)),
        ],
        compiler_params=pltpu.CompilerParams(
            collective_id=0, has_side_effects=True, vmem_limit_bytes=63 * 1024 * 1024
        ),
    )(
        tokens, routes.T, gates.T, norm_gain.reshape(1, -1),
        w_gate.reshape(eff, width), w_up.reshape(eff, width), w_down.reshape(eff, width),
    )


def takes_gathered(mesh, tokens, routes, w_gate):
    sizes = mesh.shape
    groups = sizes["role"] * sizes["expert"]
    tok, top_k, experts = tokens.shape[0] // groups, routes.shape[1], w_gate.shape[0]
    capacity = min(tok, max(2, 3 * tok * top_k // (2 * experts)))
    return (
        sizes["role"] == 2 and sizes["tensor"] == 2 and sizes["expert"] % 2 == 0
        and experts == groups and 2 * top_k >= experts and 2 * experts <= LANES
        and 4 * tok == LANES and capacity % 4 == 0 and w_gate.shape[1] % (2 * LANES) == 0
        and tokens.shape[1] % (2 * LANES) == 0
    )


def expert_ffn(arrived, w_gate, w_up, w_down):
    gate = jnp.einsum("sekq,efq->sekf", arrived, w_gate, preferred_element_type=jnp.float32)
    upward = jnp.einsum("sekq,efq->sekf", arrived, w_up, preferred_element_type=jnp.float32)
    gate, upward = lax.psum((gate, upward), "tensor")
    hidden = (jax.nn.silu(gate) * upward).astype(jnp.bfloat16)
    output = jnp.einsum("sekf,efq->sekq", hidden, w_down, preferred_element_type=jnp.float32)
    return output.astype(jnp.bfloat16)


def per_device(tokens, routes, gates, norm_gain, w_gate, w_up, w_down):
    tok_dev, quarter = tokens.shape
    top_k = routes.shape[1]
    exp_dev = w_gate.shape[0]
    n_role = lax.axis_size("role")
    n_expert = lax.axis_size("expert")
    n_tensor = lax.axis_size("tensor")
    devices = n_role * n_expert
    experts = exp_dev * devices
    capacity = min(tok_dev, max(2, 3 * tok_dev * top_k // (2 * experts)))
    width = quarter * n_tensor
    slots = experts * capacity
    picked = routes.reshape(-1)
    one_hot = (picked[:, None] == jnp.arange(experts, dtype=jnp.int32)[None, :]).astype(jnp.int32)
    running = jnp.cumsum(one_hot, axis=0) - one_hot
    earlier = jnp.sum(running * one_hot, axis=1)
    slot_ids = (picked * capacity + earlier).reshape(tok_dev, top_k)
    matches = slot_ids[:, None, :] == jnp.arange(slots, dtype=jnp.int32)[None, :, None]
    pick_rows = jnp.sum(matches.astype(jnp.float32), axis=2).astype(jnp.bfloat16)
    combine = jnp.sum(jnp.where(matches, gates[:, None, :], 0.0), axis=2)
    own = tokens.astype(jnp.float32)
    squares = lax.psum(jnp.sum(own * own, axis=1), "tensor")
    scale = lax.rsqrt(squares / width + 1e-06)[:, None]
    gain_part = lax.dynamic_slice_in_dim(norm_gain, lax.axis_index("tensor") * quarter, quarter)
    normed = (own * scale * gain_part[None, :]).astype(jnp.bfloat16)
    outgoing = jnp.einsum(
        "ts,td->sd", pick_rows, normed, preferred_element_type=jnp.float32
    ).astype(jnp.bfloat16)
    outgoing = outgoing.reshape(devices, exp_dev, capacity, quarter)
    results = expert_ffn(
        lax.all_to_all(outgoing, ("role", "expert"), split_axis=0, concat_axis=0, tiled=True),
        w_gate,
        w_up,
        w_down,
    )
    returned = lax.all_to_all(results, ("role", "expert"), split_axis=0, concat_axis=0, tiled=True)
    returned = returned.reshape(slots, quarter).astype(jnp.float32)
    mixed = jnp.dot(
        combine, returned, precision=lax.Precision.HIGHEST, preferred_element_type=jnp.float32
    )
    return mixed.astype(jnp.bfloat16)


def solution(mesh):
    in_specs = (
        P(("role", "expert"), "tensor"),
        P(("role", "expert"), None),
        P(("role", "expert"), None),
        P(),
        P(("role", "expert"), None, "tensor"),
        P(("role", "expert"), None, "tensor"),
        P(("role", "expert"), None, "tensor"),
    )
    out_specs = P(("role", "expert"), "tensor")

    def layer(tokens, routes, gates, norm_gain, w_gate, w_up, w_down):
        body = gathered if takes_gathered(mesh, tokens, routes, w_gate) else per_device
        return jax.shard_map(
            body, mesh=mesh, in_specs=in_specs, out_specs=out_specs, check_vma=False
        )(tokens, routes, gates, norm_gain, w_gate, w_up, w_down)

    return layer
```
